256 devices in a mesh: dp: 32 (over x, z), vocab: 8 (over y, core).
Axes of the slice: x: 4, y: 4, z: 8, core: 2. Of those that a mesh axis runs over, the one named last changes fastest.
Arguments:
- hidden: bfloat16 [32, 16, 8192], P('dp', 'vocab'), may hold values from -48 to 48
- targets: int32 [32, 16], P('dp', 'vocab'), may hold values from 0 to 128255
- unembed: bfloat16 [128256, 8192], P(('dp', 'vocab')), may hold values from -3 to 3
- out_proj: bfloat16 [128256, 64], P(('dp', 'vocab')), may hold values from -6 to 6
- in_proj: bfloat16 [8192, 64], replicated, may hold values from -0.0625 to 0.0625
Outputs:
- gradients: float32 [32, 4096], P('dp', 'vocab')
The draws below stay inside these ranges and needn't reach their ends.
All inputs are finite; a program needn't handle non-finite values.
Results may differ from the reference program's by a relative error of at most 0.0003.
The reference program's roundings to bfloat16 on the way (of `delta_rows`) count: a program that leaves them out, or rounds other values in their place, can miss the bound.
Values may be sent and summed in bfloat16 or wider, within the bound.
No kernel may reach another device: no remote copies, remote signals or barrier semaphores. Data moves between devices by JAX's collectives and lax.ppermute only.
A program may use at most 128 MiB of HBM per device.

```python
import math
import jax
import jax.numpy as jnp
from jax import lax

D = 8192
V = 128256
KO = 64
KI = 64
LEN = 16
EXAMPLES = 32
DEVICES = 256


def anchor_table(key):
    block_width = D // 16
    sign_first = jax.random.randint(jax.random.fold_in(key, 101), (8, block_width), 0, 2).astype(jnp.float32) * 2.0 - 1.0
    sign_second = jax.random.randint(jax.random.fold_in(key, 103), (8, block_width), 0, 2).astype(jnp.float32) * 2.0 - 1.0
    unit_scale = 1.0 / math.sqrt(block_width)
    placing = jnp.eye(16, dtype=jnp.float32)
    main_dirs = (placing[:8][:, :, None] * (sign_first * unit_scale)[:, None, :]).reshape(8, D)
    side_dirs = (placing[8:][:, :, None] * (sign_second * unit_scale)[:, None, :]).reshape(8, D)
    magnitudes = jnp.exp(jax.random.uniform(jax.random.fold_in(key, 104), (8,), jnp.float32, 0.0, math.log(3.0)))
    offset = jax.random.randint(jax.random.fold_in(key, 102), (), 0, V // 16)
    first_rows = jnp.arange(8, dtype=jnp.int32) * (2 * (V // 16)) + offset
    second_rows = first_rows + V // 16
    return (main_dirs, side_dirs, magnitudes, first_rows, second_rows)


def draw_unembed(key, part):
    main_dirs, side_dirs, magnitudes, first_rows, second_rows = anchor_table(key)
    key = jax.random.fold_in(key, 1)
    values = jax.random.normal(key, (V, D), jnp.float32) * (3.0 / math.sqrt(D))
    first_vecs = magnitudes[:, None] * main_dirs
    second_vecs = first_vecs + side_dirs
    values = values.at[first_rows].set(first_vecs)
    values = values.at[second_rows].set(second_vecs)
    return jnp.clip(values, -3.0, 3.0).astype(jnp.bfloat16)


def draw_hidden(key, part):
    key = jax.random.fold_in(key, 2)
    values = jnp.clip(jax.random.normal(jax.random.fold_in(key, 11), (EXAMPLES, LEN, D), jnp.float32), -6.0, 6.0)
    return jnp.clip(values, -48.0, 48.0).astype(jnp.bfloat16)


def with_ends(result, own_key, least, top_value):
    extent = result.shape
    place = [jax.random.randint(jax.random.fold_in(own_key, axis), (), 0, extent[axis]) for axis in range(len(extent))]
    result = result.at[tuple(place)].set(least)
    longest = extent.index(max(extent))
    place[longest] = (place[longest] + 1) % extent[longest]
    return result.at[tuple(place)].set(top_value)


def block_scale(key, extent, shards, low, top_value):
    loudness = 1.0
    for dim, shards_of in shards:
        heights = jax.random.uniform(jax.random.fold_in(jax.random.fold_in(key, 6), dim), (shards_of,), jnp.float32, low / len(shards), top_value / len(shards))
        loudness = loudness * jnp.repeat(jnp.exp(heights), extent[dim] // shards_of).reshape((-1,) + (1,) * (len(extent) - 1 - dim))
    return loudness


def scatter_about(own_key, dims, spread, limit, cuts=(), kind=jnp.bfloat16):
    entries = spread * jax.random.normal(own_key, dims, jnp.float32)
    if cuts:
        entries = entries * block_scale(own_key, dims, cuts, -0.22, 0.18)
    return jnp.clip(entries, -limit, limit).astype(kind)


def setup_inputs(seed: int = 0) -> dict:
    key_list = jax.random.split(jax.random.key(seed), 6)
    hidden = draw_hidden(jax.random.fold_in(key_list[5], 71), 0)
    targets = with_ends(jax.random.randint(key_list[1], (EXAMPLES, LEN), 0, V), jax.random.fold_in(key_list[1], 1), 0, V - 1).astype(jnp.int32)
    unembed = draw_unembed(jax.random.fold_in(key_list[5], 71), 0)
    out_proj = scatter_about(key_list[3], (V, KO), 1.0, 6.0, ((0, 256),))
    in_proj = scatter_about(key_list[4], (D, KI), D ** -0.5, 0.0625)
    return dict(hidden=hidden, targets=targets, unembed=unembed, out_proj=out_proj, in_proj=in_proj)


def reference(hidden, targets, unembed, out_proj, in_proj):
    token_count = EXAMPLES * LEN
    token_rows = hidden.reshape(token_count, D)
    target_ids = targets.reshape(token_count)
    blocks = unembed.reshape(DEVICES // 8, -1, D)

    def logit_block(weights):
        return lax.dot_general(weights, token_rows, (((1,), (1,)), ((), ())), preferred_element_type=jnp.float32)

    logits = lax.map(logit_block, blocks).reshape(V, token_count)
    col_max = jnp.max(logits, axis=0)
    col_sum = jnp.sum(jnp.exp(logits - col_max[None, :]), axis=0)
    softmax_w = jnp.exp(logits - col_max[None, :]) / col_sum[None, :]
    onehot = (jnp.arange(V, dtype=jnp.int32)[:, None] == target_ids[None, :]).astype(jnp.float32)
    delta_rows = (softmax_w - onehot).astype(jnp.bfloat16)
    out_coords = lax.dot_general(out_proj, delta_rows, (((0,), (0,)), ((), ())), preferred_element_type=jnp.float32)
    proj_rows = jnp.dot(token_rows, in_proj, preferred_element_type=jnp.float32)
    gradients = jnp.einsum("oel,eli->eoi", out_coords.reshape(KO, EXAMPLES, LEN), proj_rows.reshape(EXAMPLES, LEN, KI), precision=lax.Precision.HIGHEST)
    return gradients.reshape(EXAMPLES, KO * KI)
```

```python
import jax
import jax.numpy as jnp
import numpy as np
from jax import lax
from jax.experimental import pallas as pl
from jax.experimental.pallas import tpu as pltpu
from jax.sharding import Mesh, PartitionSpec as P

NX, NZ, NY, NC = 4, 8, 4, 2
ALL = ("x", "z", "y", "c")
GRAN = 32
KSTEPS = 8


def device_index(x, z, y, c):
    return ((x % NX * NZ + z % NZ) * NY + y % NY) * NC + c


def shift_pairs(axes, shift):
    pairs = []
    for x in range(NX):
        for z in range(NZ):
            for y in range(NY):
                for c in range(NC):
                    dx, dy = (shift, 0) if axes[c] == "x" else (0, shift)
                    pairs.append((device_index(x + dx, z, y + dy, c), device_index(x, z, y, c)))
    return pairs


def from_shift(value, axes, shift):
    return lax.ppermute(value, ALL, shift_pairs(axes, shift))


def swap_core(value):
    return lax.ppermute(value, "c", [(0, 1), (1, 0)])


def scores_kernel(core, offsets, *refs):
    blocks = refs[:8]
    u_own, u_other, in_t, own_out, other_out, rows, sems = refs[8:]
    step = pl.program_id(0)
    vocab_here = u_own.shape[0]
    width = u_own.shape[1]

    def copies():
        return [
            pltpu.make_async_copy(
                blocks[b].at[pl.ds(g * GRAN, GRAN), :],
                rows.at[pl.ds(pl.multiple_of(offsets[2 * b + g], GRAN), GRAN), :],
                sems.at[2 * b + g],
            )
            for b in range(8)
            for g in range(2)
        ]

    @pl.when(step == 0)
    def _():
        for copy in copies():
            copy.start()
        for copy in copies():
            copy.wait()
        own_out[...] = jnp.zeros_like(own_out)
        other_out[...] = jnp.zeros_like(other_out)

    piece = rows[:, pl.ds(pl.multiple_of(step * width, width), width)]

    def dot(left):
        return lax.dot_general(left, piece, (((1,), (1,)), ((), ())), preferred_element_type=jnp.float32)

    own_out[:vocab_here, :] += dot(u_own[...])
    other_out[:vocab_here, :] += dot(u_other[...])
    projected = dot(in_t[...])
    base = own_out.shape[0] - projected.shape[0]
    own_out[base:, :] += projected
    other_out[base:, :] += projected


def partial_scores(core, offsets, blocks, unembed, u_other, in_t):
    vocab_here = unembed.shape[0]
    half = u_other.shape[1]
    width = half // KSTEPS
    count = GRAN * NX * NY
    in_width = in_t.shape[0]
    out_rows = -(-vocab_here // 8) * 8 + in_width
    out = jax.ShapeDtypeStruct((out_rows, count), jnp.float32)
    return pl.pallas_call(
        scores_kernel,
        grid_spec=pltpu.PrefetchScalarGridSpec(
            num_scalar_prefetch=2,
            grid=(KSTEPS,),
            in_specs=[pl.BlockSpec(memory_space=pl.ANY)] * 8
            + [
                pl.BlockSpec((vocab_here, width), lambda k, core, offsets: (0, core[0] * KSTEPS + k)),
                pl.BlockSpec((vocab_here, width), lambda k, core, offsets: (0, k)),
                pl.BlockSpec((in_width, width), lambda k, core, offsets: (0, core[0] * KSTEPS + k)),
            ],
            out_specs=[pl.BlockSpec((out_rows, count), lambda k, core, offsets: (0, 0))] * 2,
            scratch_shapes=[pltpu.VMEM((count, half), jnp.bfloat16), pltpu.SemaphoreType.DMA((16,))],
        ),
        out_shape=[out, out],
        compiler_params=pltpu.CompilerParams(vmem_limit_bytes=40 * 2**20),
        cost_estimate=pl.CostEstimate(flops=2 * 2 * vocab_here * count * half, bytes_accessed=2 * half * (2 * vocab_here + count), transcendentals=0),
        name="partial_scores",
    )(core, offsets, *blocks, unembed, u_other, in_t)


def merge(pairs):
    top = jnp.max(pairs[:, 0], axis=0)
    total = jnp.sum(pairs[:, 1] * jnp.exp(pairs[:, 0] - top[None]), axis=0)
    return top, total


def body(hidden, targets, unembed, out_proj, in_proj):
    features = hidden.shape[2]
    half = features // 2
    vocab_here = unembed.shape[0]
    out_width = out_proj.shape[1]
    in_width = in_proj.shape[1]
    count = GRAN * NX * NY
    x, z, y, c = (lax.axis_index(a) for a in ALL)

    rows = hidden.reshape(2, features)
    keep = lax.dynamic_slice_in_dim(rows, c * half, half, 1)
    give = lax.dynamic_slice_in_dim(rows, (1 - c) * half, half, 1)
    got = swap_core(give)
    chip = jnp.where(c == 0, jnp.stack([keep, got]), jnp.stack([got, keep])).reshape(4, half)
    u_give = lax.dynamic_slice_in_dim(unembed, (1 - c) * half, half, 1)
    u_other = swap_core(u_give)

    along_z = lax.all_to_all(jnp.broadcast_to(chip[None], (NZ, 4, half)), "z", 0, 0)
    base = along_z.reshape(GRAN, half)

    first, second = ("x", "y"), ("y", "x")
    up = from_shift(base, first, 1)
    down = from_shift(base, first, -1)
    far = from_shift(base, first, 2)
    q1 = jnp.concatenate([base, up])
    q2 = jnp.concatenate([down, far])
    a = from_shift(q1, second, -1)
    b = from_shift(q2, second, 1)
    d = from_shift(q2, second, -1)
    e = from_shift(q1, second, 1)
    f = from_shift(a, second, -1)
    g = from_shift(b, second, 1)
    blocks = [q1, q2, a, b, d, e, f, g]
    places = [(0, 0), (1, 0), (0, -1), (1, 1), (1, -1), (0, 1), (0, 2), (1, 2)]
    p = jnp.where(c == 0, x, y)
    q = jnp.where(c == 0, y, x)
    offsets = []
    for which, s2 in places:
        for s1 in ((0, 1), (-1, 2))[which]:
            pp, qq = (p + s1) % 4, (q + s2) % 4
            xx, yy = jnp.where(c == 0, pp, qq), jnp.where(c == 0, qq, pp)
            offsets.append((xx * NY + yy) * GRAN)
    offsets = jnp.stack(offsets).astype(jnp.int32)
    core = c.astype(jnp.int32).reshape(1)
    own, other = partial_scores(core, offsets, blocks, unembed, u_other, in_proj.T)
    whole = own + swap_core(other)
    logits = whole[:vocab_here]
    proj = lax.dynamic_slice(
        whole[-in_width:].reshape(in_width, NX, NY, NZ, 4), (0, x, 0, z, 0), (in_width, 1, NY, 1, 4)
    ).reshape(in_width, 16)

    local_max = jnp.max(logits, axis=0)
    local_sum = jnp.sum(jnp.exp(logits - local_max[None, :]), axis=0)
    ids = jnp.pad(targets.reshape(2).astype(jnp.float32), (0, 126))
    message = jnp.concatenate([local_max, local_sum, ids])
    got = lax.all_to_all(jnp.broadcast_to(message[None], (NX * NY * NC, message.shape[0])), ("x", "y", "c"), 0, 0)
    top, total = merge(got[:, : 2 * count].reshape(-1, 2, count))
    ids = got[:, 2 * count : 2 * count + 2].reshape(64)
    message = jnp.concatenate([top, total, jnp.pad(ids, (0, 64))])
    got = lax.all_to_all(jnp.broadcast_to(message[None], (NZ, message.shape[0])), "z", 0, 0)
    col_max, col_sum = merge(got[:, : 2 * count].reshape(-1, 2, count))
    ids = got[:, 2 * count : 2 * count + 64].reshape(NZ, NX * NY, 4).transpose(1, 0, 2).reshape(count)
    ids = ids.astype(jnp.int32)

    row_ids = lax.iota(jnp.int32, vocab_here) + device_index(x, z, y, c) * vocab_here
    softmax_w = jnp.exp(logits - col_max[None, :]) / col_sum[None, :]
    onehot = (row_ids[:, None] == ids[None, :]).astype(jnp.float32)
    delta_rows = (softmax_w - onehot).astype(jnp.bfloat16)
    projected = lax.dot_general(
        out_proj, delta_rows, (((0,), (0,)), ((), ())), preferred_element_type=jnp.float32
    )
    sent = projected.reshape(8, 8, NX, NY, NZ, 4).transpose(2, 4, 0, 1, 3, 5).reshape(256, 128)
    got = lax.all_to_all(sent, ALL, 0, 0)
    coords = jnp.sum(got, axis=0).reshape(8, 16)
    grads = lax.dot_general(
        coords, proj, (((1,), (1,)), ((), ())), precision=lax.Precision.HIGHEST, preferred_element_type=jnp.float32
    )
    return grads.reshape(1, 8 * in_width)


def solution(mesh):
    wide = Mesh(np.asarray(mesh.devices).reshape(NX, NZ, NY, NC), ALL)
    dp, vocab = ("x", "z"), ("y", "c")
    return jax.shard_map(
        body,
        mesh=wide,
        in_specs=(
            P(dp, vocab, None),
            P(dp, vocab),
            P(ALL, None),
            P(ALL, None),
            P(),
        ),
        out_specs=P(dp, vocab),
        check_vma=False,
    )
```

```python
import jax
import jax.numpy as jnp
import numpy as np
from jax import lax
from jax.experimental import pallas as pl
from jax.experimental.pallas import tpu as pltpu
from jax.sharding import Mesh, PartitionSpec as P

NX, NZ, NY, NC = 4, 8, 4, 2
ALL = ("x", "z", "y", "c")
GRAN = 32
PIECE = GRAN // NC
SIDE = NX * NY * PIECE
BLOCK = 512
STEPS = 4
DIGITS = 128
CONTRACT_LAST = (((1,), (1,)), ((), ()))
CONTRACT_FIRST = (((0,), (0,)), ((), ()))
CONTRACT = (((1,), (0,)), ((), ()))
VMEM_SPEC = pl.BlockSpec(memory_space=pltpu.VMEM)
SMEM_SPEC = pl.BlockSpec(memory_space=pltpu.SMEM)
ANY_SPEC = pl.BlockSpec(memory_space=pl.ANY)
PLACES = (((0, 0), (1, 0)), ((-1, 0), (2, 0)))


def device_index(x, z, y, c):
    return ((x % NX * NZ + z % NZ) * NY + y % NY) * NC + c


def shift_pairs(axes, shift):
    pairs = []
    for x in range(NX):
        for z in range(NZ):
            for y in range(NY):
                for c in range(NC):
                    dx, dy = (shift, 0) if axes[c] == "x" else (0, shift)
                    pairs.append((device_index(x + dx, z, y + dy, c), device_index(x, z, y, c)))
    return pairs


def from_shift(value, axes, shift):
    return lax.ppermute(value, ALL, shift_pairs(axes, shift))


def swap_core(value):
    return lax.ppermute(value, "c", [(0, 1), (1, 0)])


def params(mib):
    return pltpu.CompilerParams(vmem_limit_bytes=mib * 2**20)


def scores_kernel(core, offsets, *refs):
    blocks = refs[:8]
    unembed, swapped, in_hbm, keep, give, ids, rows, u_own, u_other, in_t, row_sems, u_sems = refs[8:]
    vocab_here, half = u_own.shape
    width = half // STEPS
    in_width = in_t.shape[0]
    start = pl.multiple_of(core[0] * half, half)

    copies = []
    for k in range(STEPS):
        here = pl.ds(k * width, width)
        there = pl.ds(pl.multiple_of(start + k * width, width), width)
        cols = pl.ds(k * width, width + (DIGITS if k == STEPS - 1 else 0))
        group = [
            pltpu.make_async_copy(
                blocks[b].at[pl.ds(i * PIECE, PIECE), cols],
                rows.at[pl.ds(pl.multiple_of(offsets[4 * b + i], PIECE), PIECE), cols],
                row_sems.at[k, 4 * b + i],
            )
            for b in range(8)
            for i in range(4)
        ]
        group.append(pltpu.make_async_copy(unembed.at[:, there], u_own.at[:, here], u_sems.at[k, 0]))
        group.append(pltpu.make_async_copy(swapped.at[:, there], u_other.at[:, here], u_sems.at[k, 1]))
        group.append(pltpu.make_async_copy(in_hbm.at[:, there], in_t.at[:, here], u_sems.at[k, 2]))
        copies.append(group)
    for group in copies:
        for copy in group:
            copy.start()
    for k in range(STEPS):
        for copy in copies[k]:
            copy.wait()
        cols = slice(k * width, (k + 1) * width)
        mine, theirs = rows[:SIDE, cols], rows[SIDE:, cols]

        def put(left, right, *places):
            value = lax.dot_general(left, right, CONTRACT_LAST, preferred_element_type=jnp.float32)
            for out, base, first, size in places:
                if k == 0:
                    out[base : base + size, :] = value[first : first + size, :]
                else:
                    out[base : base + size, :] += value[first : first + size, :]

        proj = 2 * BLOCK
        both = jnp.concatenate([in_t[:, cols], u_own[:, cols]], axis=0)
        put(both, mine, (keep, 0, in_width, vocab_here), (keep, proj, 0, in_width), (give, proj + in_width, 0, in_width))
        put(both, theirs, (give, BLOCK, in_width, vocab_here), (give, proj, 0, in_width), (keep, proj + in_width, 0, in_width))
        put(u_other[:, cols], mine, (keep, BLOCK, 0, vocab_here))
        put(u_other[:, cols], theirs, (give, 0, 0, vocab_here))
    digit = lax.broadcasted_iota(jnp.int32, (8, DIGITS), 1)
    scale = jnp.where(digit == 0, 1.0, jnp.where(digit == 1, 256.0, jnp.where(digit == 2, 65536.0, 0.0)))
    ids[...] = lax.dot_general(
        scale.astype(jnp.bfloat16), rows[:SIDE, half:], CONTRACT_LAST, preferred_element_type=jnp.float32
    )


def partial_scores(core, offsets, blocks, unembed, swapped, in_t):
    vocab_here, features = unembed.shape
    half = features // 2
    in_width = in_t.shape[0]
    out = jax.ShapeDtypeStruct((2 * BLOCK + 2 * in_width, SIDE), jnp.float32)
    return pl.pallas_call(
        scores_kernel,
        in_specs=[SMEM_SPEC] * 2 + [ANY_SPEC] * 11,
        out_specs=[VMEM_SPEC] * 3,
        scratch_shapes=[
            pltpu.VMEM((2 * SIDE, half + DIGITS), jnp.bfloat16),
            pltpu.VMEM((vocab_here, half), jnp.bfloat16),
            pltpu.VMEM((vocab_here, half), jnp.bfloat16),
            pltpu.VMEM((in_width, half), jnp.bfloat16),
            pltpu.SemaphoreType.DMA((STEPS, 32)),
            pltpu.SemaphoreType.DMA((STEPS, 3)),
        ],
        out_shape=[out, out, jax.ShapeDtypeStruct((8, SIDE), jnp.float32)],
        compiler_params=params(40),
        cost_estimate=pl.CostEstimate(
            flops=2 * 2 * vocab_here * 2 * SIDE * half, bytes_accessed=2 * half * (2 * vocab_here + 2 * SIDE), transcendentals=0
        ),
        name="partial_scores",
    )(core, offsets, *blocks, unembed, swapped, in_t)


def stats_kernel(vocab_here, keep, got, logits, proj, message):
    proj[...] = keep[2 * BLOCK :, :] + got[2 * BLOCK :, :]
    top = None
    for b in range(2):
        part = slice(b * BLOCK, b * BLOCK + vocab_here)
        value = keep[part, :] + got[part, :]
        logits[part, :] = value
        here = jnp.max(value, axis=0, keepdims=True)
        top = here if top is None else jnp.maximum(top, here)
    total = jnp.zeros_like(top)
    for b in range(2):
        part = slice(b * BLOCK, b * BLOCK + vocab_here)
        total += jnp.sum(jnp.exp(logits[part, :] - top), axis=0, keepdims=True)
    lse = top + jnp.log(total)
    line = lax.broadcasted_iota(jnp.int32, message.shape, 0)
    message[...] = jnp.where(line % 2 == 0, lse[:, :128], lse[:, 128:])


def local_stats(keep, got, vocab_here):
    chips = NX * NY * NZ
    return pl.pallas_call(
        lambda *refs: stats_kernel(vocab_here, *refs),
        in_specs=[VMEM_SPEC] * 2,
        out_specs=[VMEM_SPEC] * 3,
        out_shape=[
            jax.ShapeDtypeStruct((2 * BLOCK, SIDE), jnp.float32),
            jax.ShapeDtypeStruct((keep.shape[0] - 2 * BLOCK, SIDE), jnp.float32),
            jax.ShapeDtypeStruct((2 * chips, 128), jnp.float32),
        ],
        compiler_params=params(12),
        name="local_stats",
    )(keep, got)


def delta_kernel(place, logits, got, ids, op_own, op_other, out, coords):
    vocab_here, width = op_own.shape
    chips = got.shape[0] // 2
    parts = jnp.concatenate([got[pl.ds(h, chips, stride=2), :] for h in range(2)], axis=1)
    top = jnp.max(parts, axis=0, keepdims=True)
    total = jnp.sum(jnp.exp(parts - top), axis=0, keepdims=True)
    ids = ids[:1, :].astype(jnp.int32)
    projected = jnp.zeros((width, SIDE), jnp.float32)
    row = lax.broadcasted_iota(jnp.int32, (vocab_here, SIDE), 0)
    for b, op in enumerate((op_own, op_other)):
        weight = jnp.exp(logits[b * BLOCK : b * BLOCK + vocab_here, :] - top) / total
        onehot = (row + place[b] == ids).astype(jnp.float32)
        delta = (weight - onehot).astype(jnp.bfloat16)
        projected += lax.dot_general(op[...], delta, CONTRACT_FIRST, preferred_element_type=jnp.float32)
    coords[:, :width] = projected.T
    lane = lax.broadcasted_iota(jnp.int32, (NZ, 128), 1)
    core = place[2]
    for x in range(NX):
        pieces = []
        for u in range(8):
            start = x * NY * PIECE + u * NZ
            pieces.append(coords[start : start + NZ, :])
        for r in range(8):
            line = jnp.concatenate([piece[:, 8 * r : 8 * r + 8] for piece in pieces] * 2, axis=1)
            out[r * 32 + x * NZ : r * 32 + (x + 1) * NZ, :] = jnp.where(lane // 64 == core, line, 0.0)


def delta_project(place, logits, got, ids, op_own, op_other):
    return pl.pallas_call(
        delta_kernel,
        in_specs=[SMEM_SPEC] + [VMEM_SPEC] * 5,
        out_specs=VMEM_SPEC,
        scratch_shapes=[pltpu.VMEM((SIDE, 128), jnp.float32)],
        out_shape=jax.ShapeDtypeStruct((256, 128), jnp.float32),
        compiler_params=params(12),
        name="delta_project",
    )(place, logits, got, ids, op_own, op_other)


def weights_kernel(place, proj, out):
    in_width = proj.shape[0] // 2
    core, x, z = place[0], place[1], place[2]
    lane = lax.broadcasted_iota(jnp.int32, (SIDE, 128), 1)
    t = lax.broadcasted_iota(jnp.int32, (SIDE, 128), 0)
    wanted = t == x * (NY * PIECE) + (lane // 8 % 8) * NZ + z
    mine = wanted & (lane // 64 == core)
    theirs = wanted & (lane // 64 != core)

    def pick(rows, chosen):
        return lax.dot_general(
            rows, chosen.astype(jnp.float32), CONTRACT, precision=lax.Precision.HIGHEST, preferred_element_type=jnp.float32
        )

    out[...] = pick(proj[:in_width, :], mine) + pick(proj[in_width:, :], theirs)


def finish_kernel(got, weights, out):
    in_width = weights.shape[0]
    total = jnp.sum(got[...], axis=0, keepdims=True)
    k = lax.broadcasted_iota(jnp.int32, (8, 128), 0)
    lane = lax.broadcasted_iota(jnp.int32, (8, 128), 1)
    spread = jnp.where(lane % 8 == k, jnp.broadcast_to(total, (8, 128)), 0.0)
    grads = lax.dot_general(
        spread, weights[...], CONTRACT_LAST, precision=lax.Precision.HIGHEST, preferred_element_type=jnp.float32
    )
    for i in range(8):
        out[:, i * in_width : (i + 1) * in_width] = grads[i : i + 1, :]


def own_weights(place, proj):
    return pl.pallas_call(
        weights_kernel,
        in_specs=[SMEM_SPEC, VMEM_SPEC],
        out_specs=VMEM_SPEC,
        out_shape=jax.ShapeDtypeStruct((proj.shape[0] // 2, 128), jnp.float32),
        compiler_params=params(8),
        name="own_weights",
    )(place, proj)


def finish(got, weights):
    return pl.pallas_call(
        finish_kernel,
        in_specs=[VMEM_SPEC] * 2,
        out_specs=VMEM_SPEC,
        out_shape=jax.ShapeDtypeStruct((1, 8 * weights.shape[0]), jnp.float32),
        compiler_params=params(8),
        name="finish",
    )(got, weights)


def body(hidden, targets, unembed, out_proj, in_proj):
    features = hidden.shape[2]
    half = features // 2
    vocab_here = unembed.shape[0]
    x, z, y, c = (lax.axis_index(a) for a in ALL)

    rows = hidden.reshape(2, features)
    ids = targets.reshape(2, 1)
    place = lax.broadcasted_iota(jnp.int32, (2, DIGITS), 1)
    digits = jnp.where(place == 0, ids % 256, jnp.where(place == 1, ids // 256 % 256, jnp.where(place == 2, ids // 65536, 0)))
    digits = digits.astype(jnp.bfloat16)
    keep = jnp.concatenate([lax.dynamic_slice_in_dim(rows, c * half, half, 1), digits], axis=1)
    give = jnp.concatenate([lax.dynamic_slice_in_dim(rows, (1 - c) * half, half, 1), digits], axis=1)
    got = swap_core(give)
    chip = jnp.where(c == 0, jnp.stack([keep, got]), jnp.stack([got, keep])).reshape(4, half + DIGITS)
    late_u, late_o, late_i, chip = lax.optimization_barrier((unembed, out_proj, in_proj, chip))

    along_z = lax.all_to_all(jnp.broadcast_to(chip[None], (NZ,) + chip.shape), "z", 0, 0)
    base = along_z.transpose(1, 0, 2).reshape(GRAN, half + DIGITS)

    swapped = swap_core(late_u)
    op_other = swap_core(late_o)
    in_t = late_i.T

    first, second = ("x", "y"), ("y", "x")
    up = from_shift(base, first, 1)
    down = from_shift(base, first, -1)
    far = from_shift(base, first, 2)
    q1 = jnp.concatenate([base, up])
    q2 = jnp.concatenate([down, far])
    a = from_shift(q1, second, -1)
    b = from_shift(q2, second, 1)
    d = from_shift(q2, second, -1)
    e = from_shift(q1, second, 1)
    f = from_shift(a, second, -1)
    g = from_shift(b, second, 1)
    blocks = [q1, q2, a, b, d, e, f, g]
    places = [(0, 0), (1, 0), (0, -1), (1, 1), (1, -1), (0, 1), (0, 2), (1, 2)]
    p = jnp.where(c == 0, x, y)
    q = jnp.where(c == 0, y, x)
    offsets = []
    for which, s2 in places:
        for s1 in ((0, 1), (-1, 2))[which]:
            pp, qq = (p + s1) % 4, (q + s2) % 4
            xx, yy = jnp.where(c == 0, pp, qq), jnp.where(c == 0, qq, pp)
            for side in range(NC):
                offsets.append(jnp.where(c == side, 0, SIDE) + (xx * NY + yy) * PIECE)
    offsets = jnp.stack(offsets).astype(jnp.int32)
    core = c.astype(jnp.int32).reshape(1)
    kept, given, ids = partial_scores(core, offsets, blocks, unembed, swapped, in_t)
    logits, proj, message = local_stats(kept, swap_core(given), vocab_here)

    got = lax.all_to_all(message, ("x", "y", "z"), 0, 0, tiled=True)
    weights = own_weights(jnp.stack([c, x, z]).astype(jnp.int32), proj)
    device = device_index(x, z, y, c)
    other = device_index(x, z, y, 1 - c)
    place = jnp.stack([device * vocab_here, other * vocab_here, c]).astype(jnp.int32)
    sent = delta_project(place, logits, got, ids, out_proj, op_other)
    got = lax.all_to_all(sent, ("y", "c", "x", "z"), 0, 0, tiled=True)
    return finish(got, weights)


def solution(mesh):
    wide = Mesh(np.asarray(mesh.devices).reshape(NX, NZ, NY, NC), ALL)
    dp, vocab = ("x", "z"), ("y", "c")
    return jax.shard_map(
        body,
        mesh=wide,
        in_specs=(
            P(dp, vocab, None),
            P(dp, vocab),
            P(ALL, None),
            P(ALL, None),
            P(),
        ),
        out_specs=P(dp, vocab),
        check_vma=False,
    )
```

```python
import jax
import jax.numpy as jnp
import numpy as np
from jax import lax
from jax.experimental import pallas as pl
from jax.experimental.pallas import tpu as pltpu
from jax.sharding import Mesh, PartitionSpec as P

NX, NZ, NY, NC = 4, 8, 4, 2
ALL = ("x", "z", "y", "c")
GRAN = 32
PIECE = GRAN // NC
SIDE = NX * NY * PIECE
BLOCK = 512
STEPS = 4
SPLIT = 2
AHEAD = 9
DIGITS = 128
CONTRACT_LAST = (((1,), (1,)), ((), ()))
CONTRACT_FIRST = (((0,), (0,)), ((), ()))
CONTRACT = (((1,), (0,)), ((), ()))
VMEM_SPEC = pl.BlockSpec(memory_space=pltpu.VMEM)
SMEM_SPEC = pl.BlockSpec(memory_space=pltpu.SMEM)
ANY_SPEC = pl.BlockSpec(memory_space=pl.ANY)
PLACES = (((0, 0), (1, 0)), ((-1, 0), (2, 0)))


def device_index(x, z, y, c):
    return ((x % NX * NZ + z % NZ) * NY + y % NY) * NC + c


def shift_pairs(axes, shift):
    pairs = []
    for x in range(NX):
        for z in range(NZ):
            for y in range(NY):
                for c in range(NC):
                    dx, dy = (shift, 0) if axes[c] == "x" else (0, shift)
                    pairs.append((device_index(x + dx, z, y + dy, c), device_index(x, z, y, c)))
    return pairs


def from_shift(value, axes, shift):
    return lax.ppermute(value, ALL, shift_pairs(axes, shift))


def swap_core(value):
    return lax.ppermute(value, "c", [(0, 1), (1, 0)])


def params(mib):
    return pltpu.CompilerParams(vmem_limit_bytes=mib * 2**20)


def scores_kernel(core, offsets, *refs):
    blocks = refs[:-12]
    unembed, swapped, in_hbm, keep, give, ids, rows, u_own, u_other, in_t, row_sems, u_sems = refs[-12:]
    pieces = [block.at[i] for block in blocks for i in range(block.shape[0])]
    vocab_here, half = u_own.shape
    width = half // STEPS
    in_width = in_t.shape[0]
    start = pl.multiple_of(core[0] * half, half)

    side = core[0]
    row_copies = []
    for part in range(SPLIT):
        size = half // SPLIT
        cols = pl.ds(part * size, size + (DIGITS if part == SPLIT - 1 else 0))
        row_copies.append(
            [
                pltpu.make_async_copy(piece.at[:, :, cols], rows.at[:, offsets[i], :, cols], row_sems.at[part, i])
                for i, piece in enumerate(pieces)
            ]
        )
    u_copies = []
    for k in range(STEPS):
        here = pl.ds(k * width, width)
        there = pl.ds(pl.multiple_of(start + k * width, width), width)
        u_copies.append(
            [
                pltpu.make_async_copy(unembed.at[:, there], u_own.at[:, here], u_sems.at[k, 0]),
                pltpu.make_async_copy(swapped.at[:, there], u_other.at[:, here], u_sems.at[k, 1]),
                pltpu.make_async_copy(in_hbm.at[:, there], in_t.at[:, here], u_sems.at[k, 2]),
            ]
        )
    order, last = [], []
    for k in range(STEPS):
        if k % (STEPS // SPLIT) == 0:
            order.append(row_copies[k // (STEPS // SPLIT)])
        order.append(u_copies[k])
        last.append(len(order))
    ahead = AHEAD
    for group in order[:ahead]:
        for copy in group:
            copy.start()
    ahead = min(ahead, len(order))
    waited = 0
    for k in range(STEPS):
        needed = last[k]
        while ahead < min(len(order), needed + AHEAD - 1):
            for copy in order[ahead]:
                copy.start()
            ahead += 1
        while waited < needed:
            for copy in order[waited]:
                copy.wait()
            waited += 1
        cols = slice(k * width, (k + 1) * width)
        mine = rows[side, :, :, cols].reshape(SIDE, width)
        theirs = rows[1 - side, :, :, cols].reshape(SIDE, width)

        def put(left, right, *places):
            value = lax.dot_general(left, right, CONTRACT_LAST, preferred_element_type=jnp.float32)
            for out, base, first, size in places:
                if k == 0:
                    out[base : base + size, :] = value[first : first + size, :]
                else:
                    out[base : base + size, :] += value[first : first + size, :]

        proj = 2 * BLOCK
        both = jnp.concatenate([in_t[:, cols], u_own[:, cols]], axis=0)
        put(both, mine, (keep, 0, in_width, vocab_here), (keep, proj, 0, in_width), (give, proj + in_width, 0, in_width))
        put(both, theirs, (give, BLOCK, in_width, vocab_here), (give, proj, 0, in_width), (keep, proj + in_width, 0, in_width))
        put(u_other[:, cols], mine, (keep, BLOCK, 0, vocab_here))
        put(u_other[:, cols], theirs, (give, 0, 0, vocab_here))
    digit = lax.broadcasted_iota(jnp.int32, (8, DIGITS), 1)
    scale = jnp.where(digit == 0, 1.0, jnp.where(digit == 1, 256.0, jnp.where(digit == 2, 65536.0, 0.0)))
    ids[...] = lax.dot_general(
        scale.astype(jnp.bfloat16), rows[side, :, :, half:].reshape(SIDE, DIGITS), CONTRACT_LAST, preferred_element_type=jnp.float32
    )


def partial_scores(core, offsets, blocks, unembed, swapped, in_t):
    vocab_here, features = unembed.shape
    half = features // 2
    in_width = in_t.shape[0]
    out = jax.ShapeDtypeStruct((2 * BLOCK + 2 * in_width, SIDE), jnp.float32)
    return pl.pallas_call(
        scores_kernel,
        in_specs=[SMEM_SPEC] * 2 + [ANY_SPEC] * (len(blocks) + 3),
        out_specs=[VMEM_SPEC] * 3,
        scratch_shapes=[
            pltpu.VMEM((NC, NX * NY, PIECE, half + DIGITS), jnp.bfloat16),
            pltpu.VMEM((vocab_here, half), jnp.bfloat16),
            pltpu.VMEM((vocab_here, half), jnp.bfloat16),
            pltpu.VMEM((in_width, half), jnp.bfloat16),
            pltpu.SemaphoreType.DMA((SPLIT, 16)),
            pltpu.SemaphoreType.DMA((STEPS, 3)),
        ],
        out_shape=[out, out, jax.ShapeDtypeStruct((8, SIDE), jnp.float32)],
        compiler_params=params(40),
        cost_estimate=pl.CostEstimate(
            flops=2 * 2 * vocab_here * 2 * SIDE * half, bytes_accessed=2 * half * (2 * vocab_here + 2 * SIDE), transcendentals=0
        ),
        name="partial_scores",
    )(core, offsets, *blocks, unembed, swapped, in_t)


def stats_kernel(vocab_here, keep, got, logits, proj, message):
    proj[...] = keep[2 * BLOCK :, :] + got[2 * BLOCK :, :]
    top = None
    for b in range(2):
        part = slice(b * BLOCK, b * BLOCK + vocab_here)
        value = keep[part, :] + got[part, :]
        logits[part, :] = value
        here = jnp.max(value, axis=0, keepdims=True)
        top = here if top is None else jnp.maximum(top, here)
    total = jnp.zeros_like(top)
    for b in range(2):
        part = slice(b * BLOCK, b * BLOCK + vocab_here)
        total += jnp.sum(jnp.exp(logits[part, :] - top), axis=0, keepdims=True)
    lse = top + jnp.log(total)
    line = lax.broadcasted_iota(jnp.int32, message.shape, 0)
    message[...] = jnp.where(line % 2 == 0, lse[:, :128], lse[:, 128:])


def local_stats(keep, got, vocab_here):
    chips = NX * NY * NZ
    return pl.pallas_call(
        lambda *refs: stats_kernel(vocab_here, *refs),
        in_specs=[VMEM_SPEC] * 2,
        out_specs=[VMEM_SPEC] * 3,
        out_shape=[
            jax.ShapeDtypeStruct((2 * BLOCK, SIDE), jnp.float32),
            jax.ShapeDtypeStruct((keep.shape[0] - 2 * BLOCK, SIDE), jnp.float32),
            jax.ShapeDtypeStruct((2 * chips, 128), jnp.float32),
        ],
        compiler_params=params(12),
        name="local_stats",
    )(keep, got)


def delta_kernel(place, logits, got, ids, op_own, op_other, out, coords):
    vocab_here, width = op_own.shape
    chips = got.shape[0] // 2
    parts = jnp.concatenate([got[pl.ds(h, chips, stride=2), :] for h in range(2)], axis=1)
    top = jnp.max(parts, axis=0, keepdims=True)
    total = jnp.sum(jnp.exp(parts - top), axis=0, keepdims=True)
    ids = ids[:1, :].astype(jnp.int32)
    projected = jnp.zeros((width, SIDE), jnp.float32)
    row = lax.broadcasted_iota(jnp.int32, (vocab_here, SIDE), 0)
    for b, op in enumerate((op_own, op_other)):
        weight = jnp.exp(logits[b * BLOCK : b * BLOCK + vocab_here, :] - top) / total
        onehot = (row + place[b] == ids).astype(jnp.float32)
        delta = (weight - onehot).astype(jnp.bfloat16)
        projected += lax.dot_general(op[...], delta, CONTRACT_FIRST, preferred_element_type=jnp.float32)
    coords[:, :width] = projected.T
    lane = lax.broadcasted_iota(jnp.int32, (NZ, 128), 1)
    core = place[2]
    for x in range(NX):
        pieces = []
        for u in range(8):
            start = x * NY * PIECE + u * NZ
            pieces.append(coords[start : start + NZ, :])
        for r in range(8):
            line = jnp.concatenate([piece[:, 8 * r : 8 * r + 8] for piece in pieces] * 2, axis=1)
            out[r * 32 + x * NZ : r * 32 + (x + 1) * NZ, :] = jnp.where(lane // 64 == core, line, 0.0)


def delta_project(place, logits, got, ids, op_own, op_other):
    return pl.pallas_call(
        delta_kernel,
        in_specs=[SMEM_SPEC] + [VMEM_SPEC] * 5,
        out_specs=VMEM_SPEC,
        scratch_shapes=[pltpu.VMEM((SIDE, 128), jnp.float32)],
        out_shape=jax.ShapeDtypeStruct((256, 128), jnp.float32),
        compiler_params=params(12),
        name="delta_project",
    )(place, logits, got, ids, op_own, op_other)


def weights_kernel(place, proj, out):
    in_width = proj.shape[0] // 2
    core, x, z = place[0], place[1], place[2]
    lane = lax.broadcasted_iota(jnp.int32, (SIDE, 128), 1)
    t = lax.broadcasted_iota(jnp.int32, (SIDE, 128), 0)
    wanted = t == x * (NY * PIECE) + (lane // 8 % 8) * NZ + z
    mine = wanted & (lane // 64 == core)
    theirs = wanted & (lane // 64 != core)

    def pick(rows, chosen):
        return lax.dot_general(
            rows, chosen.astype(jnp.float32), CONTRACT, precision=lax.Precision.HIGHEST, preferred_element_type=jnp.float32
        )

    out[...] = pick(proj[:in_width, :], mine) + pick(proj[in_width:, :], theirs)


def finish_kernel(got, weights, out):
    in_width = weights.shape[0]
    total = jnp.sum(got[...], axis=0, keepdims=True)
    k = lax.broadcasted_iota(jnp.int32, (8, 128), 0)
    lane = lax.broadcasted_iota(jnp.int32, (8, 128), 1)
    spread = jnp.where(lane % 8 == k, jnp.broadcast_to(total, (8, 128)), 0.0)
    grads = lax.dot_general(
        spread, weights[...], CONTRACT_LAST, precision=lax.Precision.HIGHEST, preferred_element_type=jnp.float32
    )
    for i in range(8):
        out[:, i * in_width : (i + 1) * in_width] = grads[i : i + 1, :]


def own_weights(place, proj):
    return pl.pallas_call(
        weights_kernel,
        in_specs=[SMEM_SPEC, VMEM_SPEC],
        out_specs=VMEM_SPEC,
        out_shape=jax.ShapeDtypeStruct((proj.shape[0] // 2, 128), jnp.float32),
        compiler_params=params(8),
        name="own_weights",
    )(place, proj)


def finish(got, weights):
    return pl.pallas_call(
        finish_kernel,
        in_specs=[VMEM_SPEC] * 2,
        out_specs=VMEM_SPEC,
        out_shape=jax.ShapeDtypeStruct((1, 8 * weights.shape[0]), jnp.float32),
        compiler_params=params(8),
        name="finish",
    )(got, weights)


def body(hidden, targets, unembed, out_proj, in_proj):
    features = hidden.shape[2]
    half = features // 2
    vocab_here = unembed.shape[0]
    x, z, y, c = (lax.axis_index(a) for a in ALL)

    rows = hidden.reshape(2, features)
    ids = targets.reshape(2, 1)
    place = lax.broadcasted_iota(jnp.int32, (2, DIGITS), 1)
    digits = jnp.where(place == 0, ids & 255, jnp.where(place == 1, (ids >> 8) & 255, jnp.where(place == 2, ids >> 16, 0)))
    digits = digits.astype(jnp.bfloat16)
    keep = jnp.concatenate([lax.dynamic_slice_in_dim(rows, c * half, half, 1), digits], axis=1)
    give = jnp.concatenate([lax.dynamic_slice_in_dim(rows, (1 - c) * half, half, 1), digits], axis=1)
    got = swap_core(give)
    chip = jnp.where(c == 0, jnp.stack([keep, got]), jnp.stack([got, keep])).reshape(4, half + DIGITS)
    late_u, late_o, late_i, chip = lax.optimization_barrier((unembed, out_proj, in_proj, chip))

    along_z = lax.all_to_all(jnp.broadcast_to(chip[None], (NZ,) + chip.shape), "z", 0, 0)
    base = along_z.transpose(1, 0, 2).reshape(GRAN, half + DIGITS)

    swapped = swap_core(late_u)
    op_other = swap_core(late_o)
    in_t = late_i.T

    first, second = ("x", "y"), ("y", "x")
    far = from_shift(base, first, 2)
    up = from_shift(base, first, 1)
    down = from_shift(base, first, -1)
    q1 = jnp.concatenate([base, up])
    q2 = jnp.concatenate([down, far])
    a = from_shift(q1, second, -1)
    e = from_shift(q1, second, 1)
    b1 = from_shift(down, second, 1)
    b2 = from_shift(far, second, 1)
    d = from_shift(q2, second, -1)
    a, e = lax.optimization_barrier((a, e))
    f = from_shift(a, second, -1)
    g1 = from_shift(b1, second, 1)
    g2 = from_shift(b2, second, 1)
    near, away = (0, 1), (-1, 2)
    gathered = [
        (q1, near, 0), (q2, away, 0), (a, near, -1), (e, near, 1), (b1, (-1,), 1), (b2, (2,), 1),
        (d, away, -1), (f, near, 2), (g1, (-1,), 2), (g2, (2,), 2),
    ]
    blocks = [v.reshape(-1, NC, PIECE, v.shape[1]) for v, _, _ in gathered]
    p = jnp.where(c == 0, x, y)
    q = jnp.where(c == 0, y, x)
    offsets = []
    for _, shifts, s2 in gathered:
        for s1 in shifts:
            pp, qq = (p + s1) % 4, (q + s2) % 4
            xx, yy = jnp.where(c == 0, pp, qq), jnp.where(c == 0, qq, pp)
            offsets.append(xx * NY + yy)
    offsets = jnp.stack(offsets).astype(jnp.int32)
    core = c.astype(jnp.int32).reshape(1)
    kept, given, ids = partial_scores(core, offsets, blocks, unembed, swapped, in_t)
    logits, proj, message = local_stats(kept, swap_core(given), vocab_here)

    got = lax.all_to_all(message, ("x", "y", "z"), 0, 0, tiled=True)
    weights = own_weights(jnp.stack([c, x, z]).astype(jnp.int32), proj)
    device = device_index(x, z, y, c)
    other = device_index(x, z, y, 1 - c)
    place = jnp.stack([device * vocab_here, other * vocab_here, c]).astype(jnp.int32)
    sent = delta_project(place, logits, got, ids, out_proj, op_other)
    got = lax.all_to_all(sent, ("y", "c", "x", "z"), 0, 0, tiled=True)
    return finish(got, weights)


def solution(mesh):
    wide = Mesh(np.asarray(mesh.devices).reshape(NX, NZ, NY, NC), ALL)
    dp, vocab = ("x", "z"), ("y", "c")
    return jax.shard_map(
        body,
        mesh=wide,
        in_specs=(
            P(dp, vocab, None),
            P(dp, vocab),
            P(ALL, None),
            P(ALL, None),
            P(),
        ),
        out_specs=P(dp, vocab),
        check_vma=False,
    )
```

```python
import jax
import jax.numpy as jnp
import numpy as np
from jax import lax
from jax.experimental import pallas as pl
from jax.experimental.pallas import tpu as pltpu
from jax.sharding import Mesh, PartitionSpec as P

NX, NZ, NY, NC = 4, 8, 4, 2
ALL = ("x", "z", "y", "c")
GRAN = 32
PIECE = GRAN // NC
SIDE = NX * NY * PIECE
BLOCK = 512
STEPS = 4
SPLIT = 1
DIGITS = 128
CONTRACT_LAST = (((1,), (1,)), ((), ()))
CONTRACT_FIRST = (((0,), (0,)), ((), ()))
CONTRACT = (((1,), (0,)), ((), ()))
VMEM_SPEC = pl.BlockSpec(memory_space=pltpu.VMEM)
SMEM_SPEC = pl.BlockSpec(memory_space=pltpu.SMEM)
ANY_SPEC = pl.BlockSpec(memory_space=pl.ANY)
HBM_SPEC = pl.BlockSpec(memory_space=pltpu.HBM)
PLACES = (((0, 0), (1, 0)), ((-1, 0), (2, 0)))


def device_index(x, z, y, c):
    return ((x % NX * NZ + z % NZ) * NY + y % NY) * NC + c


def shift_pairs(axes, shift):
    pairs = []
    for x in range(NX):
        for z in range(NZ):
            for y in range(NY):
                for c in range(NC):
                    dx, dy = (shift, 0) if axes[c] == "x" else (0, shift)
                    pairs.append((device_index(x + dx, z, y + dy, c), device_index(x, z, y, c)))
    return pairs


def from_shift(value, axes, shift):
    return lax.ppermute(value, ALL, shift_pairs(axes, shift))


def swap_core(value):
    return lax.ppermute(value, "c", [(0, 1), (1, 0)])


def params(mib):
    return pltpu.CompilerParams(vmem_limit_bytes=mib * 2**20)


def fetch_kernel(core, unembed, swapped, in_hbm, u_own, u_other, in_t, sems):
    half = u_own.shape[1]
    there = pl.ds(pl.multiple_of(core[0] * half, half), half)
    copies = [
        pltpu.make_async_copy(source.at[:, there], target, sems.at[i])
        for i, (source, target) in enumerate(((unembed, u_own), (swapped, u_other), (in_hbm, in_t)))
    ]
    for copy in copies:
        copy.start()
    for copy in copies:
        copy.wait()


def fetch_columns(core, unembed, swapped, in_t):
    vocab_here, features = unembed.shape
    half = features // 2
    in_width = in_t.shape[0]
    return pl.pallas_call(
        fetch_kernel,
        in_specs=[SMEM_SPEC] + [HBM_SPEC] * 3,
        out_specs=[VMEM_SPEC] * 3,
        scratch_shapes=[pltpu.SemaphoreType.DMA((3,))],
        out_shape=[
            jax.ShapeDtypeStruct((vocab_here, half), jnp.bfloat16),
            jax.ShapeDtypeStruct((vocab_here, half), jnp.bfloat16),
            jax.ShapeDtypeStruct((in_width, half), jnp.bfloat16),
        ],
        compiler_params=params(44),
        cost_estimate=pl.CostEstimate(flops=0, bytes_accessed=4 * half * (2 * vocab_here + in_width), transcendentals=0),
        name="fetch_columns",
    )(core, unembed, swapped, in_t)


def give_kernel(core, offsets, *refs):
    blocks = refs[:-6]
    u_own, u_other, in_t, give, rows, row_sems = refs[-6:]
    pieces = [block.at[i] for block in blocks for i in range(block.shape[0])]
    vocab_here, half = u_own.shape
    width = half // STEPS
    in_width = in_t.shape[0]
    side = core[0]
    copies = []
    for part in range(SPLIT):
        size = half // SPLIT
        cols = pl.ds(part * size, size + (DIGITS if part == SPLIT - 1 else 0))
        copies.append(
            [
                pltpu.make_async_copy(piece.at[:, :, cols], rows.at[:, offsets[i], :, cols], row_sems.at[part, i])
                for i, piece in enumerate(pieces)
            ]
        )
    for group in copies:
        for copy in group:
            copy.start()
    for k in range(STEPS):
        if k % (STEPS // SPLIT) == 0:
            for copy in copies[k // (STEPS // SPLIT)]:
                copy.wait()
        cols = slice(k * width, (k + 1) * width)
        theirs = rows[1 - side, :, :, cols].reshape(SIDE, width)
        both = jnp.concatenate([in_t[:, cols], u_own[:, cols]], axis=0)
        put(k, both, theirs, (give, BLOCK, in_width, vocab_here), (give, 2 * BLOCK, 0, in_width))
        put(k, u_other[:, cols], theirs, (give, 0, 0, vocab_here))


def put(k, left, right, *places):
    value = lax.dot_general(left, right, CONTRACT_LAST, preferred_element_type=jnp.float32)
    for out, base, first, size in places:
        if k == 0:
            out[base : base + size, :] = value[first : first + size, :]
        else:
            out[base : base + size, :] += value[first : first + size, :]


def keep_kernel(core, rows, u_own, u_other, in_t, keep, ids):
    vocab_here, half = u_own.shape
    width = half // STEPS
    in_width = in_t.shape[0]
    side = core[0]
    for k in range(STEPS):
        cols = slice(k * width, (k + 1) * width)
        mine = rows[side, :, :, cols].reshape(SIDE, width)
        both = jnp.concatenate([in_t[:, cols], u_own[:, cols]], axis=0)
        put(k, both, mine, (keep, 0, in_width, vocab_here), (keep, 2 * BLOCK, 0, in_width))
        put(k, u_other[:, cols], mine, (keep, BLOCK, 0, vocab_here))
    digit = lax.broadcasted_iota(jnp.int32, (8, DIGITS), 1)
    scale = jnp.where(digit == 0, 1.0, jnp.where(digit == 1, 256.0, jnp.where(digit == 2, 65536.0, 0.0)))
    ids[...] = lax.dot_general(
        scale.astype(jnp.bfloat16),
        rows[side, :, :, half:].reshape(SIDE, DIGITS),
        CONTRACT_LAST,
        preferred_element_type=jnp.float32,
    )


def keep_scores(core, rows, u_own, u_other, in_t):
    vocab_here, half = u_own.shape
    return pl.pallas_call(
        keep_kernel,
        in_specs=[SMEM_SPEC] + [VMEM_SPEC] * 4,
        out_specs=[VMEM_SPEC] * 2,
        out_shape=[
            jax.ShapeDtypeStruct((2 * BLOCK + in_t.shape[0], SIDE), jnp.float32),
            jax.ShapeDtypeStruct((8, SIDE), jnp.float32),
        ],
        compiler_params=params(4),
        cost_estimate=pl.CostEstimate(flops=2 * 2 * vocab_here * SIDE * half, bytes_accessed=2 * half * 2 * vocab_here, transcendentals=0),
        name="keep_scores",
    )(core, rows, u_own, u_other, in_t)


def give_scores(core, offsets, blocks, u_own, u_other, in_t):
    vocab_here, half = u_own.shape
    return pl.pallas_call(
        give_kernel,
        in_specs=[SMEM_SPEC] * 2 + [ANY_SPEC] * len(blocks) + [VMEM_SPEC] * 3,
        out_specs=[VMEM_SPEC] * 2,
        scratch_shapes=[pltpu.SemaphoreType.DMA((SPLIT, 16))],
        out_shape=[
            jax.ShapeDtypeStruct((2 * BLOCK + in_t.shape[0], SIDE), jnp.float32),
            jax.ShapeDtypeStruct((NC, NX * NY, PIECE, half + DIGITS), jnp.bfloat16),
        ],
        compiler_params=params(4),
        cost_estimate=pl.CostEstimate(
            flops=2 * 2 * vocab_here * SIDE * half, bytes_accessed=2 * half * (2 * vocab_here + 2 * SIDE), transcendentals=0
        ),
        name="give_scores",
    )(core, offsets, *blocks, u_own, u_other, in_t)


def stats_kernel(vocab_here, keep, got, logits, proj, message):
    proj[...] = keep[2 * BLOCK :, :] + got[2 * BLOCK :, :]
    top = None
    for b in range(2):
        part = slice(b * BLOCK, b * BLOCK + vocab_here)
        value = keep[part, :] + got[part, :]
        logits[part, :] = value
        here = jnp.max(value, axis=0, keepdims=True)
        top = here if top is None else jnp.maximum(top, here)
    total = jnp.zeros_like(top)
    for b in range(2):
        part = slice(b * BLOCK, b * BLOCK + vocab_here)
        total += jnp.sum(jnp.exp(logits[part, :] - top), axis=0, keepdims=True)
    lse = top + jnp.log(total)
    line = lax.broadcasted_iota(jnp.int32, message.shape, 0)
    message[...] = jnp.where(line % 2 == 0, lse[:, :128], lse[:, 128:])


def local_stats(keep, got, vocab_here):
    chips = NX * NY * NZ
    return pl.pallas_call(
        lambda *refs: stats_kernel(vocab_here, *refs),
        in_specs=[VMEM_SPEC] * 2,
        out_specs=[VMEM_SPEC] * 3,
        out_shape=[
            jax.ShapeDtypeStruct((2 * BLOCK, SIDE), jnp.float32),
            jax.ShapeDtypeStruct((keep.shape[0] - 2 * BLOCK, SIDE), jnp.float32),
            jax.ShapeDtypeStruct((2 * chips, 128), jnp.float32),
        ],
        compiler_params=params(12),
        name="local_stats",
    )(keep, got)


def delta_kernel(place, logits, got, ids, op_own, op_other, out, coords):
    vocab_here, width = op_own.shape
    chips = got.shape[0] // 2
    parts = jnp.concatenate([got[pl.ds(h, chips, stride=2), :] for h in range(2)], axis=1)
    top = jnp.max(parts, axis=0, keepdims=True)
    scale = 1.0 / jnp.sum(jnp.exp(parts - top), axis=0, keepdims=True)
    ids = ids[:1, :].astype(jnp.int32)
    projected = jnp.zeros((width, SIDE), jnp.float32)
    row = lax.broadcasted_iota(jnp.int32, (vocab_here, SIDE), 0)
    for b, op in enumerate((op_own, op_other)):
        weight = jnp.exp(logits[b * BLOCK : b * BLOCK + vocab_here, :] - top) * scale
        onehot = (row == ids - place[b]).astype(jnp.float32)
        delta = (weight - onehot).astype(jnp.bfloat16)
        projected += lax.dot_general(op[...], delta, CONTRACT_FIRST, preferred_element_type=jnp.float32)
    coords[:, :width] = projected.T
    lane = lax.broadcasted_iota(jnp.int32, (NZ, 128), 1)
    core = place[2]
    for x in range(NX):
        pieces = []
        for u in range(8):
            start = x * NY * PIECE + u * NZ
            pieces.append(coords[start : start + NZ, :])
        for r in range(8):
            line = jnp.concatenate([piece[:, 8 * r : 8 * r + 8] for piece in pieces] * 2, axis=1)
            out[r * 32 + x * NZ : r * 32 + (x + 1) * NZ, :] = jnp.where(lane // 64 == core, line, 0.0)


def delta_project(place, logits, got, ids, op_own, op_other):
    return pl.pallas_call(
        delta_kernel,
        in_specs=[SMEM_SPEC] + [VMEM_SPEC] * 5,
        out_specs=VMEM_SPEC,
        scratch_shapes=[pltpu.VMEM((SIDE, 128), jnp.float32)],
        out_shape=jax.ShapeDtypeStruct((256, 128), jnp.float32),
        compiler_params=params(12),
        name="delta_project",
    )(place, logits, got, ids, op_own, op_other)


def weights_kernel(place, proj, proj_other, out):
    core, x, z = place[0], place[1], place[2]
    lane = lax.broadcasted_iota(jnp.int32, (SIDE, 128), 1)
    t = lax.broadcasted_iota(jnp.int32, (SIDE, 128), 0)
    wanted = t == x * (NY * PIECE) + (lane // 8 % 8) * NZ + z
    mine = wanted & (lane // 64 == core)
    theirs = wanted & (lane // 64 != core)

    def pick(rows, chosen):
        return lax.dot_general(
            rows, chosen.astype(jnp.float32), CONTRACT, precision=lax.Precision.HIGHEST, preferred_element_type=jnp.float32
        )

    out[...] = pick(proj[...], mine) + pick(proj_other[...], theirs)


def finish_kernel(got, weights, out):
    in_width = weights.shape[0]
    total = jnp.sum(got[...], axis=0, keepdims=True)
    k = lax.broadcasted_iota(jnp.int32, (8, 128), 0)
    lane = lax.broadcasted_iota(jnp.int32, (8, 128), 1)
    spread = jnp.where(lane % 8 == k, jnp.broadcast_to(total, (8, 128)), 0.0)
    grads = lax.dot_general(
        spread, weights[...], CONTRACT_LAST, precision=lax.Precision.HIGHEST, preferred_element_type=jnp.float32
    )
    for i in range(8):
        out[:, i * in_width : (i + 1) * in_width] = grads[i : i + 1, :]


def own_weights(place, proj, proj_other):
    return pl.pallas_call(
        weights_kernel,
        in_specs=[SMEM_SPEC] + [VMEM_SPEC] * 2,
        out_specs=VMEM_SPEC,
        out_shape=jax.ShapeDtypeStruct((proj.shape[0], 128), jnp.float32),
        compiler_params=params(8),
        name="own_weights",
    )(place, proj, proj_other)


def finish(got, weights):
    return pl.pallas_call(
        finish_kernel,
        in_specs=[VMEM_SPEC] * 2,
        out_specs=VMEM_SPEC,
        out_shape=jax.ShapeDtypeStruct((1, 8 * weights.shape[0]), jnp.float32),
        compiler_params=params(8),
        name="finish",
    )(got, weights)


def body(hidden, targets, unembed, out_proj, in_proj):
    features = hidden.shape[2]
    half = features // 2
    vocab_here = unembed.shape[0]
    x, z, y, c = (lax.axis_index(a) for a in ALL)

    rows = hidden.reshape(2, features)
    ids = targets.reshape(2, 1)
    place = lax.broadcasted_iota(jnp.int32, (2, DIGITS), 1)
    digits = jnp.where(place == 0, ids & 255, jnp.where(place == 1, (ids >> 8) & 255, jnp.where(place == 2, ids >> 16, 0)))
    digits = digits.astype(jnp.bfloat16)
    keep = lax.dynamic_slice_in_dim(rows, c * half, half, 1)
    got = swap_core(lax.dynamic_slice_in_dim(rows, (1 - c) * half, half, 1))
    keep = jnp.concatenate([keep, digits], axis=1)
    got = jnp.pad(got, ((0, 0), (0, DIGITS)))
    chip = jnp.where(c == 0, jnp.stack([keep, got]), jnp.stack([got, keep])).reshape(4, half + DIGITS)
    late_u, late_o, late_i, chip = lax.optimization_barrier((unembed, out_proj, in_proj, chip))

    along_z = lax.all_to_all(jnp.broadcast_to(chip[None], (NZ,) + chip.shape), "z", 0, 0)
    base = along_z.transpose(1, 0, 2).reshape(GRAN, half + DIGITS)

    swapped = swap_core(late_u)
    op_other = swap_core(late_o)
    in_t = late_i.T

    first, second = ("x", "y"), ("y", "x")
    far = from_shift(base, first, 2)
    up = from_shift(base, first, 1)
    down = from_shift(base, first, -1)
    q1 = jnp.concatenate([base, up])
    q2 = jnp.concatenate([down, far])
    a = from_shift(q1, second, -1)
    e = from_shift(q1, second, 1)
    b1 = from_shift(down, second, 1)
    b2 = from_shift(far, second, 1)
    d = from_shift(q2, second, -1)
    a, e = lax.optimization_barrier((a, e))
    f = from_shift(a, second, -1)
    g1 = from_shift(b1, second, 1)
    g2 = from_shift(b2, second, 1)
    near, away = (0, 1), (-1, 2)
    gathered = [
        (q1, near, 0), (q2, away, 0), (a, near, -1), (e, near, 1), (b1, (-1,), 1), (b2, (2,), 1),
        (d, away, -1), (f, near, 2), (g1, (-1,), 2), (g2, (2,), 2),
    ]
    blocks = [v.reshape(-1, NC, PIECE, v.shape[1]) for v, _, _ in gathered]
    p = jnp.where(c == 0, x, y)
    q = jnp.where(c == 0, y, x)
    offsets = []
    for _, shifts, s2 in gathered:
        for s1 in shifts:
            pp, qq = (p + s1) % 4, (q + s2) % 4
            xx, yy = jnp.where(c == 0, pp, qq), jnp.where(c == 0, qq, pp)
            offsets.append(xx * NY + yy)
    offsets = jnp.stack(offsets).astype(jnp.int32)
    core = c.astype(jnp.int32).reshape(1)
    held = fetch_columns(core, unembed, swapped, in_t)
    given, gathered = give_scores(core, offsets, blocks, *held)
    got = swap_core(given)
    kept, ids = keep_scores(core, gathered, *held)
    logits, proj, message = local_stats(kept, got, vocab_here)

    got = lax.all_to_all(message, ("x", "y", "z"), 0, 0, tiled=True)
    weights = own_weights(jnp.stack([c, x, z]).astype(jnp.int32), proj, swap_core(proj))
    device = device_index(x, z, y, c)
    other = device_index(x, z, y, 1 - c)
    place = jnp.stack([device * vocab_here, other * vocab_here, c]).astype(jnp.int32)
    sent = delta_project(place, logits, got, ids, out_proj, op_other)
    got = lax.all_to_all(sent, ("y", "c", "x", "z"), 0, 0, tiled=True)
    return finish(got, weights)


def solution(mesh):
    wide = Mesh(np.asarray(mesh.devices).reshape(NX, NZ, NY, NC), ALL)
    dp, vocab = ("x", "z"), ("y", "c")
    return jax.shard_map(
        body,
        mesh=wide,
        in_specs=(
            P(dp, vocab, None),
            P(dp, vocab),
            P(ALL, None),
            P(ALL, None),
            P(),
        ),
        out_specs=P(dp, vocab),
        check_vma=False,
    )
```

```python
import jax
import jax.numpy as jnp
import numpy as np
from jax import lax
from jax.experimental import pallas as pl
from jax.experimental.pallas import tpu as pltpu
from jax.sharding import Mesh, PartitionSpec as P

NX, NZ, NY, NC = 4, 8, 4, 2
ALL = ("x", "z", "y", "c")
GRAN = 32
PIECE = GRAN // NC
SIDE = NX * NY * PIECE
BLOCK = 512
STEPS = 4
SPLIT = 1
DIGITS = 128
CONTRACT_LAST = (((1,), (1,)), ((), ()))
CONTRACT_FIRST = (((0,), (0,)), ((), ()))
CONTRACT = (((1,), (0,)), ((), ()))
VMEM_SPEC = pl.BlockSpec(memory_space=pltpu.VMEM)
SMEM_SPEC = pl.BlockSpec(memory_space=pltpu.SMEM)
ANY_SPEC = pl.BlockSpec(memory_space=pl.ANY)
HBM_SPEC = pl.BlockSpec(memory_space=pltpu.HBM)
PLACES = (((0, 0), (1, 0)), ((-1, 0), (2, 0)))


def device_index(x, z, y, c):
    return ((x % NX * NZ + z % NZ) * NY + y % NY) * NC + c


def shift_pairs(axes, shift):
    pairs = []
    for x in range(NX):
        for z in range(NZ):
            for y in range(NY):
                for c in range(NC):
                    dx, dy = (shift, 0) if axes[c] == "x" else (0, shift)
                    pairs.append((device_index(x + dx, z, y + dy, c), device_index(x, z, y, c)))
    return pairs


def from_shift(value, axes, shift):
    return lax.ppermute(value, ALL, shift_pairs(axes, shift))


def swap_core(value):
    return lax.ppermute(value, "c", [(0, 1), (1, 0)])


def params(mib):
    return pltpu.CompilerParams(vmem_limit_bytes=mib * 2**20)


def fetch_kernel(core, unembed, swapped, in_hbm, u_own, u_other, in_t, sems):
    half = u_own.shape[1]
    there = pl.ds(pl.multiple_of(core[0] * half, half), half)
    copies = [
        pltpu.make_async_copy(source.at[:, there], target, sems.at[i])
        for i, (source, target) in enumerate(((unembed, u_own), (swapped, u_other), (in_hbm, in_t)))
    ]
    for copy in copies:
        copy.start()
    for copy in copies:
        copy.wait()


def fetch_columns(core, unembed, swapped, in_t):
    vocab_here, features = unembed.shape
    half = features // 2
    in_width = in_t.shape[0]
    return pl.pallas_call(
        fetch_kernel,
        in_specs=[SMEM_SPEC] + [HBM_SPEC] * 3,
        out_specs=[VMEM_SPEC] * 3,
        scratch_shapes=[pltpu.SemaphoreType.DMA((3,))],
        out_shape=[
            jax.ShapeDtypeStruct((vocab_here, half), jnp.bfloat16),
            jax.ShapeDtypeStruct((vocab_here, half), jnp.bfloat16),
            jax.ShapeDtypeStruct((in_width, half), jnp.bfloat16),
        ],
        compiler_params=params(44),
        cost_estimate=pl.CostEstimate(flops=0, bytes_accessed=4 * half * (2 * vocab_here + in_width), transcendentals=0),
        name="fetch_columns",
    )(core, unembed, swapped, in_t)


def give_kernel(core, offsets, *refs):
    blocks = refs[:-6]
    u_own, u_other, in_t, give, rows, row_sems = refs[-6:]
    pieces = [block.at[i] for block in blocks for i in range(block.shape[0])]
    vocab_here, half = u_own.shape
    width = half // STEPS
    in_width = in_t.shape[0]
    side = core[0]
    copies = []
    for part in range(SPLIT):
        size = half // SPLIT
        cols = pl.ds(part * size, size + (DIGITS if part == SPLIT - 1 else 0))
        copies.append(
            [
                pltpu.make_async_copy(piece.at[:, :, cols], rows.at[:, offsets[i], :, cols], row_sems.at[part, i])
                for i, piece in enumerate(pieces)
            ]
        )
    for group in copies:
        for copy in group:
            copy.start()
    for k in range(STEPS):
        if k % (STEPS // SPLIT) == 0:
            for copy in copies[k // (STEPS // SPLIT)]:
                copy.wait()
        cols = slice(k * width, (k + 1) * width)
        theirs = rows[1 - side, :, :, cols].reshape(SIDE, width)
        both = jnp.concatenate([in_t[:, cols], u_own[:, cols]], axis=0)
        put(k, both, theirs, (give, BLOCK, in_width, vocab_here), (give, 2 * BLOCK, 0, in_width))
        put(k, u_other[:, cols], theirs, (give, 0, 0, vocab_here))


def put(k, left, right, *places):
    value = lax.dot_general(left, right, CONTRACT_LAST, preferred_element_type=jnp.float32)
    for out, base, first, size in places:
        if k == 0:
            out[base : base + size, :] = value[first : first + size, :]
        else:
            out[base : base + size, :] += value[first : first + size, :]


def keep_kernel(core, rows, u_own, u_other, in_t, keep, ids):
    vocab_here, half = u_own.shape
    width = half // STEPS
    in_width = in_t.shape[0]
    side = core[0]
    for k in range(STEPS):
        cols = slice(k * width, (k + 1) * width)
        mine = rows[side, :, :, cols].reshape(SIDE, width)
        both = jnp.concatenate([in_t[:, cols], u_own[:, cols]], axis=0)
        put(k, both, mine, (keep, 0, in_width, vocab_here), (keep, 2 * BLOCK, 0, in_width))
        put(k, u_other[:, cols], mine, (keep, BLOCK, 0, vocab_here))
    digit = lax.broadcasted_iota(jnp.int32, (8, DIGITS), 1)
    scale = jnp.where(digit == 0, 1.0, jnp.where(digit == 1, 256.0, jnp.where(digit == 2, 65536.0, 0.0)))
    ids[...] = lax.dot_general(
        scale.astype(jnp.bfloat16),
        rows[side, :, :, half:].reshape(SIDE, DIGITS),
        CONTRACT_LAST,
        preferred_element_type=jnp.float32,
    )


def keep_scores(core, rows, u_own, u_other, in_t):
    vocab_here, half = u_own.shape
    return pl.pallas_call(
        keep_kernel,
        in_specs=[SMEM_SPEC] + [VMEM_SPEC] * 4,
        out_specs=[VMEM_SPEC] * 2,
        out_shape=[
            jax.ShapeDtypeStruct((2 * BLOCK + in_t.shape[0], SIDE), jnp.float32),
            jax.ShapeDtypeStruct((8, SIDE), jnp.float32),
        ],
        compiler_params=params(4),
        cost_estimate=pl.CostEstimate(flops=2 * 2 * vocab_here * SIDE * half, bytes_accessed=2 * half * 2 * vocab_here, transcendentals=0),
        name="keep_scores",
    )(core, rows, u_own, u_other, in_t)


def give_scores(core, offsets, blocks, u_own, u_other, in_t):
    vocab_here, half = u_own.shape
    return pl.pallas_call(
        give_kernel,
        in_specs=[SMEM_SPEC] * 2 + [ANY_SPEC] * len(blocks) + [VMEM_SPEC] * 3,
        out_specs=[VMEM_SPEC] * 2,
        scratch_shapes=[pltpu.SemaphoreType.DMA((SPLIT, 16))],
        out_shape=[
            jax.ShapeDtypeStruct((2 * BLOCK + in_t.shape[0], SIDE), jnp.float32),
            jax.ShapeDtypeStruct((NC, NX * NY, PIECE, half + DIGITS), jnp.bfloat16),
        ],
        compiler_params=params(4),
        cost_estimate=pl.CostEstimate(
            flops=2 * 2 * vocab_here * SIDE * half, bytes_accessed=2 * half * (2 * vocab_here + 2 * SIDE), transcendentals=0
        ),
        name="give_scores",
    )(core, offsets, *blocks, u_own, u_other, in_t)


def stats_kernel(vocab_here, keep, got, logits, proj, message):
    proj[...] = keep[2 * BLOCK :, :] + got[2 * BLOCK :, :]
    top = None
    for b in range(2):
        part = slice(b * BLOCK, b * BLOCK + vocab_here)
        value = keep[part, :] + got[part, :]
        logits[part, :] = value
        here = jnp.max(value, axis=0, keepdims=True)
        top = here if top is None else jnp.maximum(top, here)
    total = jnp.zeros_like(top)
    for b in range(2):
        part = slice(b * BLOCK, b * BLOCK + vocab_here)
        total += jnp.sum(jnp.exp(logits[part, :] - top), axis=0, keepdims=True)
    lse = top + jnp.log(total)
    line = lax.broadcasted_iota(jnp.int32, message.shape, 0)
    message[...] = jnp.where(line % 2 == 0, lse[:, :128], lse[:, 128:])


def local_stats(keep, got, vocab_here):
    chips = NX * NY * NZ
    return pl.pallas_call(
        lambda *refs: stats_kernel(vocab_here, *refs),
        in_specs=[VMEM_SPEC] * 2,
        out_specs=[VMEM_SPEC] * 3,
        out_shape=[
            jax.ShapeDtypeStruct((2 * BLOCK, SIDE), jnp.float32),
            jax.ShapeDtypeStruct((keep.shape[0] - 2 * BLOCK, SIDE), jnp.float32),
            jax.ShapeDtypeStruct((2 * chips, 128), jnp.float32),
        ],
        compiler_params=params(12),
        name="local_stats",
    )(keep, got)


def delta_kernel(place, logits, got, ids, op_own, op_other, out, coords):
    vocab_here, width = op_own.shape
    chips = got.shape[0] // 2
    parts = jnp.concatenate([got[pl.ds(h, chips, stride=2), :] for h in range(2)], axis=1)
    top = jnp.max(parts, axis=0, keepdims=True)
    scale = 1.0 / jnp.sum(jnp.exp(parts - top), axis=0, keepdims=True)
    ids = ids[:1, :].astype(jnp.int32)
    projected = jnp.zeros((width, SIDE), jnp.float32)
    row = lax.broadcasted_iota(jnp.int32, (vocab_here, SIDE), 0)
    for b, op in enumerate((op_own, op_other)):
        weight = jnp.exp(logits[b * BLOCK : b * BLOCK + vocab_here, :] - top) * scale
        onehot = (row == ids - place[b]).astype(jnp.float32)
        delta = (weight - onehot).astype(jnp.bfloat16)
        projected += lax.dot_general(op[...], delta, CONTRACT_FIRST, preferred_element_type=jnp.float32)
    coords[:, :width] = projected.T
    coords[:, width:] = jnp.zeros((SIDE, 128 - width), jnp.float32)
    core = place[2]
    coords[...] = pltpu.roll(coords[...], core * width, 1)
    group = lax.broadcasted_iota(jnp.int32, (NZ, 128), 1) // 8 - core * 8
    chosen = [group == u for u in range(8)]
    for x in range(NX):
        pieces = []
        for u in range(8):
            start = x * NY * PIECE + u * NZ
            pieces.append(coords[start : start + NZ, :])
        for r in range(8):
            line = jnp.zeros((NZ, 128), jnp.float32)
            for u in range(8):
                moved = pieces[u] if u == r else pltpu.roll(pieces[u], (u - r) * 8 % 128, 1)
                line = jnp.where(chosen[u], moved, line)
            out[r * 32 + x * NZ : r * 32 + (x + 1) * NZ, :] = line


def delta_project(place, logits, got, ids, op_own, op_other):
    return pl.pallas_call(
        delta_kernel,
        in_specs=[SMEM_SPEC] + [VMEM_SPEC] * 5,
        out_specs=VMEM_SPEC,
        scratch_shapes=[pltpu.VMEM((SIDE, 128), jnp.float32)],
        out_shape=jax.ShapeDtypeStruct((256, 128), jnp.float32),
        compiler_params=params(12),
        name="delta_project",
    )(place, logits, got, ids, op_own, op_other)


def weights_kernel(place, proj, proj_other, out):
    core, x, z = place[0], place[1], place[2]
    lane = lax.broadcasted_iota(jnp.int32, (SIDE, 128), 1)
    t = lax.broadcasted_iota(jnp.int32, (SIDE, 128), 0)
    wanted = t == x * (NY * PIECE) + (lane // 8 % 8) * NZ + z
    mine = wanted & (lane // 64 == core)
    theirs = wanted & (lane // 64 != core)

    def pick(rows, chosen):
        return lax.dot_general(
            rows, chosen.astype(jnp.float32), CONTRACT, precision=lax.Precision.HIGHEST, preferred_element_type=jnp.float32
        )

    out[...] = pick(proj[...], mine) + pick(proj_other[...], theirs)


def finish_kernel(got, weights, out):
    in_width = weights.shape[0]
    total = jnp.sum(got[...], axis=0, keepdims=True)
    k = lax.broadcasted_iota(jnp.int32, (8, 128), 0)
    lane = lax.broadcasted_iota(jnp.int32, (8, 128), 1)
    spread = jnp.where(lane % 8 == k, jnp.broadcast_to(total, (8, 128)), 0.0)
    grads = lax.dot_general(
        spread, weights[...], CONTRACT_LAST, precision=lax.Precision.HIGHEST, preferred_element_type=jnp.float32
    )
    for i in range(8):
        out[:, i * in_width : (i + 1) * in_width] = grads[i : i + 1, :]


def own_weights(place, proj, proj_other):
    return pl.pallas_call(
        weights_kernel,
        in_specs=[SMEM_SPEC] + [VMEM_SPEC] * 2,
        out_specs=VMEM_SPEC,
        out_shape=jax.ShapeDtypeStruct((proj.shape[0], 128), jnp.float32),
        compiler_params=params(8),
        name="own_weights",
    )(place, proj, proj_other)


def finish(got, weights):
    return pl.pallas_call(
        finish_kernel,
        in_specs=[VMEM_SPEC] * 2,
        out_specs=VMEM_SPEC,
        out_shape=jax.ShapeDtypeStruct((1, 8 * weights.shape[0]), jnp.float32),
        compiler_params=params(8),
        name="finish",
    )(got, weights)


def body(hidden, targets, unembed, out_proj, in_proj):
    features = hidden.shape[2]
    half = features // 2
    vocab_here = unembed.shape[0]
    x, z, y, c = (lax.axis_index(a) for a in ALL)

    rows = hidden.reshape(2, features)
    ids = targets.reshape(2, 1)
    place = lax.broadcasted_iota(jnp.int32, (2, DIGITS), 1)
    digits = jnp.where(place == 0, ids & 255, jnp.where(place == 1, (ids >> 8) & 255, jnp.where(place == 2, ids >> 16, 0)))
    digits = digits.astype(jnp.bfloat16)
    keep = lax.dynamic_slice_in_dim(rows, c * half, half, 1)
    got = swap_core(lax.dynamic_slice_in_dim(rows, (1 - c) * half, half, 1))
    keep = jnp.concatenate([keep, digits], axis=1)
    got = jnp.pad(got, ((0, 0), (0, DIGITS)))
    chip = jnp.where(c == 0, jnp.stack([keep, got]), jnp.stack([got, keep])).reshape(4, half + DIGITS)
    late_u, late_o, late_i, chip = lax.optimization_barrier((unembed, out_proj, in_proj, chip))

    along_z = lax.all_to_all(jnp.broadcast_to(chip[None], (NZ,) + chip.shape), "z", 0, 0)
    base = along_z.transpose(1, 0, 2).reshape(GRAN, half + DIGITS)

    swapped = swap_core(late_u)
    op_other = swap_core(late_o)
    in_t = late_i.T

    first, second = ("x", "y"), ("y", "x")
    far = from_shift(base, first, 2)
    up = from_shift(base, first, 1)
    down = from_shift(base, first, -1)
    q1 = jnp.concatenate([base, up])
    q2 = jnp.concatenate([down, far])
    a = from_shift(q1, second, -1)
    e = from_shift(q1, second, 1)
    b1 = from_shift(down, second, 1)
    b2 = from_shift(far, second, 1)
    d = from_shift(q2, second, -1)
    a, e = lax.optimization_barrier((a, e))
    f = from_shift(a, second, -1)
    g1 = from_shift(b1, second, 1)
    g2 = from_shift(b2, second, 1)
    near, away = (0, 1), (-1, 2)
    gathered = [
        (q1, near, 0), (q2, away, 0), (a, near, -1), (e, near, 1), (b1, (-1,), 1), (b2, (2,), 1),
        (d, away, -1), (f, near, 2), (g1, (-1,), 2), (g2, (2,), 2),
    ]
    blocks = [v.reshape(-1, NC, PIECE, v.shape[1]) for v, _, _ in gathered]
    p = jnp.where(c == 0, x, y)
    q = jnp.where(c == 0, y, x)
    offsets = []
    for _, shifts, s2 in gathered:
        for s1 in shifts:
            pp, qq = (p + s1) % 4, (q + s2) % 4
            xx, yy = jnp.where(c == 0, pp, qq), jnp.where(c == 0, qq, pp)
            offsets.append(xx * NY + yy)
    offsets = jnp.stack(offsets).astype(jnp.int32)
    core = c.astype(jnp.int32).reshape(1)
    held = fetch_columns(core, unembed, swapped, in_t)
    given, gathered = give_scores(core, offsets, blocks, *held)
    got = swap_core(given)
    kept, ids = keep_scores(core, gathered, *held)
    logits, proj, message = local_stats(kept, got, vocab_here)

    got = lax.all_to_all(message, ("x", "y", "z"), 0, 0, tiled=True)
    weights = own_weights(jnp.stack([c, x, z]).astype(jnp.int32), proj, swap_core(proj))
    device = device_index(x, z, y, c)
    other = device_index(x, z, y, 1 - c)
    place = jnp.stack([device * vocab_here, other * vocab_here, c]).astype(jnp.int32)
    sent = delta_project(place, logits, got, ids, out_proj, op_other)
    got = lax.all_to_all(sent, ("y", "c", "x", "z"), 0, 0, tiled=True)
    return finish(got, weights)


def solution(mesh):
    wide = Mesh(np.asarray(mesh.devices).reshape(NX, NZ, NY, NC), ALL)
    dp, vocab = ("x", "z"), ("y", "c")
    return jax.shard_map(
        body,
        mesh=wide,
        in_specs=(
            P(dp, vocab, None),
            P(dp, vocab),
            P(ALL, None),
            P(ALL, None),
            P(),
        ),
        out_specs=P(dp, vocab),
        check_vma=False,
    )
```
